32 devices in a mesh: groups: 2 (over y), cent: 4 (over z), pts: 4 (over x, core).
Axes of the slice: x: 2, y: 2, z: 4, core: 2. Of those that a mesh axis runs over, the one named last changes fastest.
Arguments:
- points: bfloat16 [4096, 1024], P(('groups', 'pts')), parts along dimension 0, may hold values from -12 to 12
- centres: bfloat16 [16384, 1024], P(('groups', 'cent')), parts along dimension 0, may hold values from -12 to 12
- alpha: float32 [16384], P(('groups', 'cent')), parts along dimension 0, may hold values from -30160460 to 30160460
Outputs:
- grads: float32 [4096, 1024], P(('groups', 'pts'), 'cent'), parts along dimension 0
- agop: float32 [2048, 1024], P(('groups', 'cent'), 'pts'), parts along dimension 0
The draws below stay inside these ranges and needn't reach their ends.
There are 2 independent parts, one for each index of `groups`. The reference program is written for one: setup_inputs(seed, part) draws one part's arguments, and reference() takes and returns one part's arrays. A program takes and returns all parts, laid end to end along the dimension named above; each array names one. Nothing has to cross between parts.
All inputs are finite; a program needn't handle non-finite values.
Results may differ from the reference program's by a relative error of at most 0.002.
Values sent between devices are 32-bit elements; how exact they have to be, the bound alone decides.
A program may use at most 64 MiB of HBM per device.

```python
import jax
import jax.numpy as jnp
from jax import lax

D = 1024
CEN_DEV = 2048
PTS = 2048
CENTRES = 8192
N_CENT = 4


def shard_levels(key, shape, cuts, smallest, top_value):
    def one(position, blocks):
        steps = jax.random.uniform(jax.random.fold_in(jax.random.fold_in(key, 6), position), (blocks,), jnp.float32, smallest / len(cuts), top_value / len(cuts))
        return jnp.repeat(jnp.exp(steps), shape[position] // blocks).reshape((-1,) + (1,) * (len(shape) - position - 1))

    loudness = one(*cuts[0])
    for cut in cuts[1:]:
        loudness = loudness * one(*cut)
    return loudness


def gaussian(own_key, dims, spread, reach, cuts=(), held_as=jnp.bfloat16):
    drawn = spread * jax.random.normal(own_key, dims, jnp.float32)
    if cuts:
        drawn = drawn * shard_levels(own_key, dims, cuts, -0.22, 0.18)
    return jnp.clip(drawn, -reach, reach).astype(held_as)


def setup_inputs(seed: int = 0, part: int = 0) -> dict:
    key_list = jax.random.split(jax.random.key(seed), 4)
    part_splits = jax.random.split(jax.random.fold_in(key_list[3], part), 4)
    return {
        "points": gaussian(part_splits[0], (PTS, D), (2.0 * (D / 1024) ** 0.25), 12.0, ((0, 4),)),
        "centres": gaussian(part_splits[1], (CENTRES, D), (2.0 * (D / 1024) ** 0.25), 12.0, ((0, 4),)),
        "alpha": gaussian(part_splits[2], (CENTRES,), (D * 2.718281828 ** (16 * (D / 1024) ** 0.5) / (20 * (D / 1024) ** 0.25 * CENTRES ** 0.5)), 30160460, ((0, 4),), jnp.float32),
    }


def reference(points, centres, alpha):
    xf = points.astype(jnp.float32)
    pnorm = jnp.sum(xf * xf, axis=1)
    zblocks = centres.reshape(N_CENT, CEN_DEV, D)
    ablocks = alpha.reshape(N_CENT, CEN_DEV)

    def step(total, block):
        zpart, apart = block
        zf = zpart.astype(jnp.float32)
        cross = jnp.dot(points, zpart.T, preferred_element_type=jnp.float32)
        dist = pnorm[:, None] + jnp.sum(zf * zf, axis=1)[None, :] - 2.0 * cross
        weight = apart[None, :] * jnp.exp(-2.0 * dist / D)
        wlow = weight.astype(jnp.bfloat16)
        term = jnp.dot(wlow, zpart, preferred_element_type=jnp.float32) - jnp.sum(weight, axis=1)[:, None] * xf
        return total + term, None

    start = jnp.zeros((PTS, D), jnp.float32)
    summed, unused = lax.scan(step, start, (zblocks, ablocks))
    grads = summed * (4.0 / D)
    agop = jnp.dot(grads.T, grads, precision=lax.Precision.HIGHEST, preferred_element_type=jnp.float32) / PTS
    return grads, agop
```

```python
import functools

import jax
import jax.numpy as jnp
from jax import lax
from jax.experimental import pallas as pl
from jax.experimental.pallas import tpu as pltpu
from jax.sharding import PartitionSpec as P

MESH = pl.DeviceIdType.MESH
PIECES = 4
GROUP = 2
TILE = 512


def kernel(n, total_pts, x_ref, z_ref, alpha_ref, grads_ref, agop_ref,
           part, from_left, from_right, gall, acc, cnorm, wlow, t_core, t_own, t_x,
           send_r, send_l, recv_r, recv_l, gsend_r, gsend_l, grecv, tsend, trecv, *, pieces):
    me = lax.axis_index("cent")
    p = lax.axis_index("pts")
    chip, core = p // 2, lax.rem(p, 2)
    rows, width = x_ref.shape
    centres = z_ref.shape[0]
    rb = rows // pieces
    cols = width // n
    right = {"cent": jnp.minimum(me + 1, n - 1)}
    left = {"cent": jnp.maximum(me - 1, 0)}
    other_core = {"pts": chip * 2 + 1 - core}
    other_chip = {"pts": (1 - chip) * 2 + core}
    has_left, has_right = me > 0, me < n - 1

    def copy(src, dst, send, recv, target):
        return pltpu.make_async_remote_copy(
            src_ref=src, dst_ref=dst, send_sem=send, recv_sem=recv,
            device_id=target, device_id_type=MESH)

    def sum_r(r, d):
        return copy(part.at[r, d], from_left.at[r, d], send_r.at[r, d], recv_r.at[r, d], right)

    def sum_l(r, d):
        return copy(part.at[r, d], from_right.at[r, d], send_l.at[r, d], recv_l.at[r, d], left)

    def gather_r(r, s):
        return copy(gall.at[r, s], gall.at[r, s], gsend_r.at[r, s], grecv.at[r, s], right)

    def gather_l(r, s):
        return copy(gall.at[r, s], gall.at[r, s], gsend_l.at[r, s], grecv.at[r, s], left)

    barrier = pltpu.get_barrier_semaphore()

    @pl.when(has_left)
    def _():
        pl.semaphore_signal(barrier, inc=1, device_id=left, device_id_type=MESH)

    @pl.when(has_right)
    def _():
        pl.semaphore_signal(barrier, inc=1, device_id=right, device_id_type=MESH)

    pl.semaphore_signal(barrier, inc=1, device_id=other_core, device_id_type=MESH)
    pl.semaphore_signal(barrier, inc=1, device_id=other_chip, device_id_type=MESH)

    @pl.loop(0, centres // 128)
    def _(i):
        at = pl.ds(pl.multiple_of(i * 128, 128), 128)
        zf = z_ref[at, :].astype(jnp.float32)
        sq = zf * zf
        lanes = sq[:, 0:128]
        for k in range(1, width // 128):
            lanes = lanes + sq[:, k * 128:(k + 1) * 128]
        cnorm[0:1, at] = jnp.sum(lanes.T, axis=0, keepdims=True)

    acc[...] = jnp.zeros_like(acc)

    def compute(g, waited):
        gr = GROUP * rb
        here = pl.ds(g * gr, gr)
        xf = x_ref[here, :].astype(jnp.float32)
        pnorm = jnp.sum(xf * xf, axis=1, keepdims=True)

        def tile(i, wsum):
            at = pl.ds(pl.multiple_of(i * TILE, TILE), TILE)
            cross = lax.dot_general(
                x_ref[here, :], z_ref[at, :], (((1,), (1,)), ((), ())),
                preferred_element_type=jnp.float32)
            dist = pnorm + cnorm[0:1, at] - 2.0 * cross
            weight = alpha_ref[0:1, at] * jnp.exp(dist * (-2.0 / width))
            wlow[:, at] = weight.astype(jnp.bfloat16)
            return wsum + jnp.sum(weight, axis=1, keepdims=True)

        wsum = lax.fori_loop(0, centres // TILE, tile, jnp.zeros((gr, 1), jnp.float32))
        if not waited:
            pl.semaphore_wait(barrier, 2 + has_left.astype(jnp.int32) + has_right.astype(jnp.int32))

        @pl.loop(0, n)
        def _(k):
            d = jnp.where(me * 2 < n, n - 1 - k, k)
            at = pl.ds(pl.multiple_of(d * cols, cols), cols)
            term = jnp.dot(wlow[...], z_ref[:, at], preferred_element_type=jnp.float32)
            term = term - wsum * x_ref[here, at].astype(jnp.float32)
            for j in range(GROUP):
                r = g * GROUP + j
                part[r, d] = term[j * rb:(j + 1) * rb]

                @pl.when((me == 0) & (d > 0))
                def _():
                    sum_r(r, d).start()

                @pl.when((me == n - 1) & (d < n - 1))
                def _():
                    sum_l(r, d).start()

    def scatter(r):
        for k in range(n):
            d = n - 1 - k

            @pl.when(has_left & (me < d))
            def _():
                sum_r(r, d).wait_recv()
                part[r, d] = part[r, d] + from_left[r, d]
                sum_r(r, d).start()

            @pl.when(has_right & (me > k))
            def _():
                sum_l(r, k).wait_recv()
                part[r, k] = part[r, k] + from_right[r, k]
                sum_l(r, k).start()

        @pl.when(has_left)
        def _():
            sum_r(r, me).wait_recv()
            part[r, me] = part[r, me] + from_left[r, me]

        @pl.when(has_right)
        def _():
            sum_l(r, me).wait_recv()
            part[r, me] = part[r, me] + from_right[r, me]

        mine = part[r, me] * (4.0 / width)
        gall[r, me] = mine
        grads_ref[r * rb:(r + 1) * rb, :] = mine

        @pl.when(has_right)
        def _():
            gather_r(r, me).start()

        @pl.when(has_left)
        def _():
            gather_l(r, me).start()

    def gather(r):
        for k in range(n):
            s = n - 1 - k

            @pl.when(me > s)
            def _():
                gather_r(r, s).wait_recv()

                @pl.when(has_right)
                def _():
                    gather_r(r, s).start()

            @pl.when(me < k)
            def _():
                gather_l(r, k).wait_recv()

                @pl.when(has_left)
                def _():
                    gather_l(r, k).start()

        @pl.loop(0, n)
        def _(s):
            acc[s] = acc[s] + lax.dot_general(
                gall[r, me], gall[r, s], (((0,), (0,)), ((), ())),
                precision=lax.Precision.HIGHEST, preferred_element_type=jnp.float32)

    for g in range(pieces // GROUP):
        compute(g, g > 0)
    for r in range(pieces):
        scatter(r)
        if r > 0:
            gather(r - 1)
    gather(pieces - 1)

    far, near = (1 - chip) * 2, chip * 2
    one = copy(acc.at[far + 1 - core], t_core, tsend.at[0], trecv.at[0], other_core)
    two = copy(acc.at[near + 1 - core], t_own, tsend.at[1], trecv.at[1], other_core)
    three = copy(acc.at[far + core], t_x, tsend.at[2], trecv.at[2], other_chip)
    one.start()
    two.start()
    one.wait_recv()
    acc[far + core] = acc[far + core] + t_core[...]
    three.start()
    two.wait_recv()
    own = acc[near + core] + t_own[...]
    three.wait_recv()
    agop_ref[...] = (own + t_x[...]) / total_pts

    one.wait_send()
    two.wait_send()
    three.wait_send()
    for r in range(pieces):
        for d in range(n):
            @pl.when(has_right & (me < d))
            def _():
                sum_r(r, d).wait_send()

            @pl.when(has_left & (me > d))
            def _():
                sum_l(r, d).wait_send()

            @pl.when(has_right & (me >= d))
            def _():
                gather_r(r, d).wait_send()

            @pl.when(has_left & (me <= d))
            def _():
                gather_l(r, d).wait_send()


def fused(n, total_pts, points, centres, alpha):
    rows, width = points.shape
    cols, cen = width // n, centres.shape[0]
    rb = rows // PIECES
    chunks = pltpu.VMEM((PIECES, n, rb, cols), jnp.float32)
    block = pltpu.VMEM((cols, cols), jnp.float32)
    sems = pltpu.SemaphoreType.DMA((PIECES, n))
    vmem = pl.BlockSpec(memory_space=pltpu.VMEM)
    return pl.pallas_call(
        functools.partial(kernel, n, float(total_pts), pieces=PIECES),
        out_shape=(
            jax.ShapeDtypeStruct((rows, cols), jnp.float32),
            jax.ShapeDtypeStruct((cols, cols), jnp.float32),
        ),
        in_specs=[vmem] * 3,
        out_specs=(vmem, vmem),
        scratch_shapes=[
            chunks, chunks, chunks, chunks,
            pltpu.VMEM((n, cols, cols), jnp.float32),
            pltpu.VMEM((8, cen), jnp.float32),
            pltpu.VMEM((GROUP * rb, cen), jnp.bfloat16),
            block, block, block,
            sems, sems, sems, sems, sems, sems, sems,
            pltpu.SemaphoreType.DMA((3,)),
            pltpu.SemaphoreType.DMA((3,)),
        ],
        compiler_params=pltpu.CompilerParams(
            collective_id=0, has_side_effects=True, vmem_limit_bytes=48 * 1024 * 1024),
        cost_estimate=pl.CostEstimate(
            flops=4 * rows * width * cen, bytes_accessed=8 * 1024 * 1024,
            transcendentals=rows * cen),
    )(points, centres, alpha.reshape(1, cen))


def plain(total_pts, points, centres, alpha):
    width = points.shape[1]
    xf = points.astype(jnp.float32)
    zf = centres.astype(jnp.float32)
    pnorm = jnp.sum(xf * xf, axis=1)
    cross = jnp.dot(points, centres.T, preferred_element_type=jnp.float32)
    dist = pnorm[:, None] + jnp.sum(zf * zf, axis=1)[None, :] - 2.0 * cross
    weight = alpha[None, :] * jnp.exp(-2.0 * dist / width)
    wlow = weight.astype(jnp.bfloat16)
    partial_grad = (
        jnp.dot(wlow, centres, preferred_element_type=jnp.float32)
        - jnp.sum(weight, axis=1)[:, None] * xf
    )
    mine = lax.psum_scatter(partial_grad, "cent", scatter_dimension=1, tiled=True) * (4.0 / width)
    outer_rows = jnp.dot(
        mine.T,
        lax.all_gather(mine, "cent", axis=1, tiled=True),
        precision=lax.Precision.HIGHEST,
        preferred_element_type=jnp.float32,
    )
    agop = lax.psum_scatter(outer_rows, "pts", scatter_dimension=1, tiled=True) / total_pts
    return (mine, agop)


def solution(mesh):
    n, npts = mesh.shape["cent"], mesh.shape["pts"]

    def per_device(points, centres, alpha):
        rows, width = points.shape
        total_pts = rows * npts
        fits = (n == npts == 4 and width % (128 * n) == 0
                and rows % (16 * PIECES) == 0 and centres.shape[0] % TILE == 0)
        if fits:
            return fused(n, total_pts, points, centres, alpha)
        return plain(total_pts, points, centres, alpha)

    in_specs = (P(("groups", "pts"), None), P(("groups", "cent"), None), P(("groups", "cent")))
    out_specs = (P(("groups", "pts"), "cent"), P(("groups", "cent"), "pts"))
    return jax.shard_map(
        per_device, mesh=mesh, in_specs=in_specs, out_specs=out_specs, check_vma=False
    )
```

```python
import functools

import jax
import jax.numpy as jnp
from jax import lax
from jax.experimental import pallas as pl
from jax.experimental.pallas import tpu as pltpu
from jax.sharding import PartitionSpec as P

MESH = pl.DeviceIdType.MESH
PIECES = 2
GROUP = 1
AHEAD = 2
LAG = 1
TILE = 512


def kernel(n, total_pts, x_ref, z_ref, alpha_ref, grads_ref, agop_ref,
           part, from_left, from_right, gall, acc, cnorm, wlow, t_core, t_own, t_x,
           send_r, send_l, recv_r, recv_l, gsend_r, gsend_l, grecv, tsend, trecv, *, pieces):
    me = lax.axis_index("cent")
    p = lax.axis_index("pts")
    chip, core = p // 2, lax.rem(p, 2)
    rows, width = x_ref.shape
    centres = z_ref.shape[0]
    rb = rows // pieces
    cols = width // n
    right = {"cent": jnp.minimum(me + 1, n - 1)}
    left = {"cent": jnp.maximum(me - 1, 0)}
    other_core = {"pts": chip * 2 + 1 - core}
    other_chip = {"pts": (1 - chip) * 2 + core}
    has_left, has_right = me > 0, me < n - 1

    def copy(src, dst, send, recv, target):
        return pltpu.make_async_remote_copy(
            src_ref=src, dst_ref=dst, send_sem=send, recv_sem=recv,
            device_id=target, device_id_type=MESH)

    def sum_r(r, d):
        return copy(part.at[r, d], from_left.at[r, d], send_r.at[r, d], recv_r.at[r, d], right)

    def sum_l(r, d):
        return copy(part.at[r, d], from_right.at[r, d], send_l.at[r, d], recv_l.at[r, d], left)

    def gather_r(r, s):
        return copy(gall.at[r, s], gall.at[r, s], gsend_r.at[r, s], grecv.at[r, s], right)

    def gather_l(r, s):
        return copy(gall.at[r, s], gall.at[r, s], gsend_l.at[r, s], grecv.at[r, s], left)

    barrier = pltpu.get_barrier_semaphore()

    @pl.when(has_left)
    def _():
        pl.semaphore_signal(barrier, inc=1, device_id=left, device_id_type=MESH)

    @pl.when(has_right)
    def _():
        pl.semaphore_signal(barrier, inc=1, device_id=right, device_id_type=MESH)

    pl.semaphore_signal(barrier, inc=1, device_id=other_core, device_id_type=MESH)
    pl.semaphore_signal(barrier, inc=1, device_id=other_chip, device_id_type=MESH)

    @pl.loop(0, centres // 128)
    def _(i):
        at = pl.ds(pl.multiple_of(i * 128, 128), 128)
        zf = z_ref[at, :].astype(jnp.float32)
        sq = zf * zf
        lanes = sq[:, 0:128]
        for k in range(1, width // 128):
            lanes = lanes + sq[:, k * 128:(k + 1) * 128]
        cnorm[0:1, at] = jnp.sum(lanes.T, axis=0, keepdims=True)

    acc[...] = jnp.zeros_like(acc)

    def begin(r, d):
        @pl.when((me == 0) & (d > 0))
        def _():
            sum_r(r, d).start()

        @pl.when((me == n - 1) & (d < n - 1))
        def _():
            sum_l(r, d).start()

    def compute(g, waited):
        gr = GROUP * rb
        here = pl.ds(g * gr, gr)
        xf = x_ref[here, :].astype(jnp.float32)
        pnorm = jnp.sum(xf * xf, axis=1, keepdims=True)

        def tile(i, wsum):
            at = pl.ds(pl.multiple_of(i * TILE, TILE), TILE)
            cross = lax.dot_general(
                x_ref[here, :], z_ref[at, :], (((1,), (1,)), ((), ())),
                preferred_element_type=jnp.float32)
            dist = pnorm + cnorm[0:1, at] - 2.0 * cross
            weight = alpha_ref[0:1, at] * jnp.exp(dist * (-2.0 / width))
            wlow[:, at] = weight.astype(jnp.bfloat16)
            return wsum + jnp.sum(weight, axis=1, keepdims=True)

        wsum = lax.fori_loop(0, centres // TILE, tile, jnp.zeros((gr, 1), jnp.float32))
        if not waited:
            pl.semaphore_wait(barrier, 2 + has_left.astype(jnp.int32) + has_right.astype(jnp.int32))

        @pl.loop(0, n)
        def _(k):
            d = jnp.where(me * 2 < n, n - 1 - k, k)
            at = pl.ds(pl.multiple_of(d * cols, cols), cols)
            term = jnp.dot(wlow[...], z_ref[:, at], preferred_element_type=jnp.float32)
            term = term - wsum * x_ref[here, at].astype(jnp.float32)
            for j in range(GROUP):
                r = g * GROUP + j
                part[r, d] = term[j * rb:(j + 1) * rb]

                if r < AHEAD:
                    begin(r, d)

    def scatter(r):
        for k in range(n):
            d = n - 1 - k

            @pl.when(has_left & (me < d))
            def _():
                sum_r(r, d).wait_recv()
                part[r, d] = part[r, d] + from_left[r, d]
                sum_r(r, d).start()

            @pl.when(has_right & (me > k))
            def _():
                sum_l(r, k).wait_recv()
                part[r, k] = part[r, k] + from_right[r, k]
                sum_l(r, k).start()

        @pl.when(has_left)
        def _():
            sum_r(r, me).wait_recv()
            part[r, me] = part[r, me] + from_left[r, me]

        @pl.when(has_right)
        def _():
            sum_l(r, me).wait_recv()
            part[r, me] = part[r, me] + from_right[r, me]

        mine = part[r, me] * (4.0 / width)
        gall[r, me] = mine
        grads_ref[r * rb:(r + 1) * rb, :] = mine

        @pl.when(has_right)
        def _():
            gather_r(r, me).start()

        @pl.when(has_left)
        def _():
            gather_l(r, me).start()

    def gather(r):
        for k in range(n):
            s = n - 1 - k

            @pl.when(me > s)
            def _():
                gather_r(r, s).wait_recv()

                @pl.when(has_right)
                def _():
                    gather_r(r, s).start()

            @pl.when(me < k)
            def _():
                gather_l(r, k).wait_recv()

                @pl.when(has_left)
                def _():
                    gather_l(r, k).start()

        if r % 2 == 0:
            return
        rows_me = gall[r - 1:r + 1, me].reshape(2 * rb, cols)

        @pl.loop(0, n)
        def _(s):
            acc[s] = acc[s] + lax.dot_general(
                rows_me, gall[r - 1:r + 1, s].reshape(2 * rb, cols), (((0,), (0,)), ((), ())),
                precision=lax.Precision.HIGHEST, preferred_element_type=jnp.float32)

    compute(0, False)
    for r in range(pieces + LAG):
        if r == 0:
            compute(1, True)
        if r < pieces:
            scatter(r)
            if r + AHEAD < pieces:
                for k in range(n):
                    begin(r + AHEAD, jnp.where(me == 0, n - 1 - k, k))
        if r >= LAG:
            gather(r - LAG)

    far, near = (1 - chip) * 2, chip * 2
    one = copy(acc.at[far + 1 - core], t_core, tsend.at[0], trecv.at[0], other_core)
    two = copy(acc.at[near + 1 - core], t_own, tsend.at[1], trecv.at[1], other_core)
    three = copy(acc.at[far + core], t_x, tsend.at[2], trecv.at[2], other_chip)
    one.start()
    two.start()
    one.wait_recv()
    acc[far + core] = acc[far + core] + t_core[...]
    three.start()
    two.wait_recv()
    own = acc[near + core] + t_own[...]
    three.wait_recv()
    agop_ref[...] = (own + t_x[...]) / total_pts

    one.wait_send()
    two.wait_send()
    three.wait_send()
    for r in range(pieces):
        for d in range(n):
            @pl.when(has_right & (me < d))
            def _():
                sum_r(r, d).wait_send()

            @pl.when(has_left & (me > d))
            def _():
                sum_l(r, d).wait_send()

            @pl.when(has_right & (me >= d))
            def _():
                gather_r(r, d).wait_send()

            @pl.when(has_left & (me <= d))
            def _():
                gather_l(r, d).wait_send()


def fused(n, total_pts, points, centres, alpha):
    rows, width = points.shape
    cols, cen = width // n, centres.shape[0]
    rb = rows // PIECES
    chunks = pltpu.VMEM((PIECES, n, rb, cols), jnp.float32)
    block = pltpu.VMEM((cols, cols), jnp.float32)
    sems = pltpu.SemaphoreType.DMA((PIECES, n))
    vmem = pl.BlockSpec(memory_space=pltpu.VMEM)
    return pl.pallas_call(
        functools.partial(kernel, n, float(total_pts), pieces=PIECES),
        out_shape=(
            jax.ShapeDtypeStruct((rows, cols), jnp.float32),
            jax.ShapeDtypeStruct((cols, cols), jnp.float32),
        ),
        in_specs=[vmem] * 3,
        out_specs=(vmem, vmem),
        scratch_shapes=[
            chunks, chunks, chunks, chunks,
            pltpu.VMEM((n, cols, cols), jnp.float32),
            pltpu.VMEM((8, cen), jnp.float32),
            pltpu.VMEM((GROUP * rb, cen), jnp.bfloat16),
            block, block, block,
            sems, sems, sems, sems, sems, sems, sems,
            pltpu.SemaphoreType.DMA((3,)),
            pltpu.SemaphoreType.DMA((3,)),
        ],
        compiler_params=pltpu.CompilerParams(
            collective_id=0, has_side_effects=True, vmem_limit_bytes=48 * 1024 * 1024),
        cost_estimate=pl.CostEstimate(
            flops=4 * rows * width * cen, bytes_accessed=8 * 1024 * 1024,
            transcendentals=rows * cen),
    )(points, centres, alpha.reshape(1, cen))


def plain(total_pts, points, centres, alpha):
    width = points.shape[1]
    xf = points.astype(jnp.float32)
    zf = centres.astype(jnp.float32)
    pnorm = jnp.sum(xf * xf, axis=1)
    cross = jnp.dot(points, centres.T, preferred_element_type=jnp.float32)
    dist = pnorm[:, None] + jnp.sum(zf * zf, axis=1)[None, :] - 2.0 * cross
    weight = alpha[None, :] * jnp.exp(-2.0 * dist / width)
    wlow = weight.astype(jnp.bfloat16)
    partial_grad = (
        jnp.dot(wlow, centres, preferred_element_type=jnp.float32)
        - jnp.sum(weight, axis=1)[:, None] * xf
    )
    mine = lax.psum_scatter(partial_grad, "cent", scatter_dimension=1, tiled=True) * (4.0 / width)
    outer_rows = jnp.dot(
        mine.T,
        lax.all_gather(mine, "cent", axis=1, tiled=True),
        precision=lax.Precision.HIGHEST,
        preferred_element_type=jnp.float32,
    )
    agop = lax.psum_scatter(outer_rows, "pts", scatter_dimension=1, tiled=True) / total_pts
    return (mine, agop)


def solution(mesh):
    n, npts = mesh.shape["cent"], mesh.shape["pts"]

    def per_device(points, centres, alpha):
        rows, width = points.shape
        total_pts = rows * npts
        fits = (n == npts == 4 and width % (128 * n) == 0
                and rows % (16 * PIECES) == 0 and centres.shape[0] % TILE == 0)
        if fits:
            return fused(n, total_pts, points, centres, alpha)
        return plain(total_pts, points, centres, alpha)

    in_specs = (P(("groups", "pts"), None), P(("groups", "cent"), None), P(("groups", "cent")))
    out_specs = (P(("groups", "pts"), "cent"), P(("groups", "cent"), "pts"))
    return jax.shard_map(
        per_device, mesh=mesh, in_specs=in_specs, out_specs=out_specs, check_vma=False
    )
```

```python
import functools

import jax
import jax.numpy as jnp
from jax import lax
from jax.experimental import pallas as pl
from jax.experimental.pallas import tpu as pltpu
from jax.sharding import PartitionSpec as P

MESH = pl.DeviceIdType.MESH
PIECES = 2
GROUP = 1
AHEAD = 2
LAG = 1
TILE = 512


def kernel(n, total_pts, x_ref, z_ref, alpha_ref, grads_ref, agop_ref,
           part, from_left, from_right, gall, acc, cnorm, wlow, t_core, t_own, t_x, t_send, t_mirror,
           send_r, send_l, recv_r, recv_l, gsend_r, gsend_l, grecv, tsend, trecv, *, pieces):
    me = lax.axis_index("cent")
    p = lax.axis_index("pts")
    chip, core = p // 2, lax.rem(p, 2)
    rows, width = x_ref.shape
    centres = z_ref.shape[0]
    rb = rows // pieces
    cols = width // n
    right = {"cent": jnp.minimum(me + 1, n - 1)}
    left = {"cent": jnp.maximum(me - 1, 0)}
    other_core = {"pts": chip * 2 + 1 - core}
    mirror = {"cent": p, "pts": me}
    other_chip = {"pts": (1 - chip) * 2 + core}
    has_left, has_right = me > 0, me < n - 1

    def here_made(s):
        return (me == s) | (has_left & ((s == 0) | (s > me)))

    def copy(src, dst, send, recv, target):
        return pltpu.make_async_remote_copy(
            src_ref=src, dst_ref=dst, send_sem=send, recv_sem=recv,
            device_id=target, device_id_type=MESH)

    def sum_r(r, d):
        return copy(part.at[r, d], from_left.at[r, d], send_r.at[r, d], recv_r.at[r, d], right)

    def sum_l(r, d):
        return copy(part.at[r, d], from_right.at[r, d], send_l.at[r, d], recv_l.at[r, d], left)

    def gather_r(r, s):
        return copy(gall.at[r, s], gall.at[r, s], gsend_r.at[r, s], grecv.at[r, s], right)

    def gather_l(r, s):
        return copy(gall.at[r, s], gall.at[r, s], gsend_l.at[r, s], grecv.at[r, s], left)

    barrier = pltpu.get_barrier_semaphore()

    @pl.when(has_left)
    def _():
        pl.semaphore_signal(barrier, inc=1, device_id=left, device_id_type=MESH)

    @pl.when(has_right)
    def _():
        pl.semaphore_signal(barrier, inc=1, device_id=right, device_id_type=MESH)

    pl.semaphore_signal(barrier, inc=1, device_id=other_core, device_id_type=MESH)
    pl.semaphore_signal(barrier, inc=1, device_id=other_chip, device_id_type=MESH)

    @pl.when(me != p)
    def _():
        pl.semaphore_signal(barrier, inc=1, device_id=mirror, device_id_type=MESH)

    @pl.loop(0, centres // 128)
    def _(i):
        at = pl.ds(pl.multiple_of(i * 128, 128), 128)
        zf = z_ref[at, :].astype(jnp.float32)
        sq = zf * zf
        lanes = sq[:, 0:128]
        for k in range(1, width // 128):
            lanes = lanes + sq[:, k * 128:(k + 1) * 128]
        cnorm[0:1, at] = jnp.sum(lanes.T, axis=0, keepdims=True)

    acc[...] = jnp.zeros_like(acc)

    def begin(r, d):
        @pl.when((me == 0) & (d > 0))
        def _():
            sum_r(r, d).start()

        @pl.when((me == n - 1) & (d < n - 1))
        def _():
            sum_l(r, d).start()

    def compute(g, waited):
        gr = GROUP * rb
        here = pl.ds(g * gr, gr)
        xf = x_ref[here, :].astype(jnp.float32)
        pnorm = jnp.sum(xf * xf, axis=1, keepdims=True)

        def tile(i, wsum):
            at = pl.ds(pl.multiple_of(i * TILE, TILE), TILE)
            cross = lax.dot_general(
                x_ref[here, :], z_ref[at, :], (((1,), (1,)), ((), ())),
                preferred_element_type=jnp.float32)
            dist = pnorm + cnorm[0:1, at] - 2.0 * cross
            weight = alpha_ref[0:1, at] * jnp.exp(dist * (-2.0 / width))
            wlow[:, at] = weight.astype(jnp.bfloat16)
            return wsum + jnp.sum(weight, axis=1, keepdims=True)

        wsum = lax.fori_loop(0, centres // TILE, tile, jnp.zeros((gr, 1), jnp.float32))
        if not waited:
            pl.semaphore_wait(barrier, 2 + has_left.astype(jnp.int32) + has_right.astype(jnp.int32)
                              + (me != p).astype(jnp.int32))

        @pl.loop(0, n)
        def _(k):
            d = jnp.where(me * 2 < n, n - 1 - k, k)
            at = pl.ds(pl.multiple_of(d * cols, cols), cols)
            term = jnp.dot(wlow[...], z_ref[:, at], preferred_element_type=jnp.float32)
            term = term - wsum * x_ref[here, at].astype(jnp.float32)
            for j in range(GROUP):
                r = g * GROUP + j
                part[r, d] = term[j * rb:(j + 1) * rb]

                if r < AHEAD:
                    begin(r, d)

    def scatter(r):
        for k in range(n):
            d = n - 1 - k

            @pl.when(has_left & (me < d))
            def _():
                sum_r(r, d).wait_recv()
                part[r, d] = part[r, d] + from_left[r, d]
                sum_r(r, d).start()

            @pl.when(has_right & (me > k))
            def _():
                sum_l(r, k).wait_recv()
                part[r, k] = part[r, k] + from_right[r, k]
                sum_l(r, k).start()

        @pl.when(has_left)
        def _():
            sum_r(r, me).wait_recv()
            part[r, me] = part[r, me] + from_left[r, me]

        @pl.when(has_right)
        def _():
            sum_l(r, me).wait_recv()
            part[r, me] = part[r, me] + from_right[r, me]

        mine = part[r, me] * (4.0 / width)
        gall[r, me] = mine
        grads_ref[r * rb:(r + 1) * rb, :] = mine

        @pl.when(me == 0)
        def _():
            gather_r(r, me).start()

        @pl.when(me > 1)
        def _():
            gather_l(r, me).start()

    def gather(r):
        @pl.when(has_left)
        def _():
            gather_r(r, 0).wait_recv()

            @pl.when(has_right)
            def _():
                gather_r(r, 0).start()

        for k in range(2, n):
            @pl.when(has_left & (me < k))
            def _():
                gather_l(r, k).wait_recv()

                @pl.when(me > 1)
                def _():
                    gather_l(r, k).start()

        if r % 2 == 0:
            return
        rows_me = gall[r - 1:r + 1, me].reshape(2 * rb, cols)

        @pl.loop(0, n)
        def _(s):
            @pl.when(here_made(s))
            def _():
                acc[s] = acc[s] + lax.dot_general(
                    rows_me, gall[r - 1:r + 1, s].reshape(2 * rb, cols), (((0,), (0,)), ((), ())),
                    precision=lax.Precision.HIGHEST, preferred_element_type=jnp.float32)

    compute(0, False)
    for r in range(pieces + LAG):
        if r == 0:
            compute(1, True)
        if r < pieces:
            scatter(r)
            if r + AHEAD < pieces:
                for k in range(n):
                    begin(r + AHEAD, jnp.where(me == 0, n - 1 - k, k))
        if r >= LAG:
            gather(r - LAG)

    far, near = (1 - chip) * 2, chip * 2
    one = copy(acc.at[far + 1 - core], t_core, tsend.at[0], trecv.at[0], other_core)
    two = copy(acc.at[near + 1 - core], t_own, tsend.at[1], trecv.at[1], other_core)
    three = copy(acc.at[far + core], t_x, tsend.at[2], trecv.at[2], other_chip)
    four = copy(t_send, t_mirror, tsend.at[3], trecv.at[3], mirror)

    @pl.when(here_made(far + 1 - core))
    def _():
        one.start()

    @pl.when(here_made(near + 1 - core))
    def _():
        two.start()

    @pl.when(here_made(far + core))
    def _():
        one.wait_recv()
        acc[far + core] = acc[far + core] + t_core[...]
        three.start()

    @pl.when(here_made(p))
    def _():
        two.wait_recv()
        own = acc[p] + t_own[...]
        three.wait_recv()
        own = (own + t_x[...]) / total_pts
        agop_ref[...] = own

        @pl.when(me != p)
        def _():
            t_send[...] = own.T
            four.start()
            four.wait_send()

    @pl.when(jnp.logical_not(here_made(p)))
    def _():
        four.wait_recv()
        agop_ref[...] = t_mirror[...]

    @pl.when(here_made(far + 1 - core))
    def _():
        one.wait_send()

    @pl.when(here_made(near + 1 - core))
    def _():
        two.wait_send()

    @pl.when(here_made(far + core))
    def _():
        three.wait_send()

    for r in range(pieces):
        for d in range(n):
            @pl.when(has_right & (me < d))
            def _():
                sum_r(r, d).wait_send()

            @pl.when(has_left & (me > d))
            def _():
                sum_l(r, d).wait_send()

            if d == 0:
                @pl.when(has_right)
                def _():
                    gather_r(r, d).wait_send()

            @pl.when((me > 1) & (me <= d))
            def _():
                gather_l(r, d).wait_send()


def fused(n, total_pts, points, centres, alpha):
    rows, width = points.shape
    cols, cen = width // n, centres.shape[0]
    rb = rows // PIECES
    chunks = pltpu.VMEM((PIECES, n, rb, cols), jnp.float32)
    block = pltpu.VMEM((cols, cols), jnp.float32)
    sems = pltpu.SemaphoreType.DMA((PIECES, n))
    vmem = pl.BlockSpec(memory_space=pltpu.VMEM)
    return pl.pallas_call(
        functools.partial(kernel, n, float(total_pts), pieces=PIECES),
        out_shape=(
            jax.ShapeDtypeStruct((rows, cols), jnp.float32),
            jax.ShapeDtypeStruct((cols, cols), jnp.float32),
        ),
        in_specs=[vmem] * 3,
        out_specs=(vmem, vmem),
        scratch_shapes=[
            chunks, chunks, chunks, chunks,
            pltpu.VMEM((n, cols, cols), jnp.float32),
            pltpu.VMEM((8, cen), jnp.float32),
            pltpu.VMEM((GROUP * rb, cen), jnp.bfloat16),
            block, block, block, block, block,
            sems, sems, sems, sems, sems, sems, sems,
            pltpu.SemaphoreType.DMA((4,)),
            pltpu.SemaphoreType.DMA((4,)),
        ],
        compiler_params=pltpu.CompilerParams(
            collective_id=0, has_side_effects=True, vmem_limit_bytes=48 * 1024 * 1024),
        cost_estimate=pl.CostEstimate(
            flops=4 * rows * width * cen, bytes_accessed=8 * 1024 * 1024,
            transcendentals=rows * cen),
    )(points, centres, alpha.reshape(1, cen))


def plain(total_pts, points, centres, alpha):
    width = points.shape[1]
    xf = points.astype(jnp.float32)
    zf = centres.astype(jnp.float32)
    pnorm = jnp.sum(xf * xf, axis=1)
    cross = jnp.dot(points, centres.T, preferred_element_type=jnp.float32)
    dist = pnorm[:, None] + jnp.sum(zf * zf, axis=1)[None, :] - 2.0 * cross
    weight = alpha[None, :] * jnp.exp(-2.0 * dist / width)
    wlow = weight.astype(jnp.bfloat16)
    partial_grad = (
        jnp.dot(wlow, centres, preferred_element_type=jnp.float32)
        - jnp.sum(weight, axis=1)[:, None] * xf
    )
    mine = lax.psum_scatter(partial_grad, "cent", scatter_dimension=1, tiled=True) * (4.0 / width)
    outer_rows = jnp.dot(
        mine.T,
        lax.all_gather(mine, "cent", axis=1, tiled=True),
        precision=lax.Precision.HIGHEST,
        preferred_element_type=jnp.float32,
    )
    agop = lax.psum_scatter(outer_rows, "pts", scatter_dimension=1, tiled=True) / total_pts
    return (mine, agop)


def solution(mesh):
    n, npts = mesh.shape["cent"], mesh.shape["pts"]

    def per_device(points, centres, alpha):
        rows, width = points.shape
        total_pts = rows * npts
        fits = (n == npts == 4 and width % (128 * n) == 0
                and rows % (16 * PIECES) == 0 and centres.shape[0] % TILE == 0)
        if fits:
            return fused(n, total_pts, points, centres, alpha)
        return plain(total_pts, points, centres, alpha)

    in_specs = (P(("groups", "pts"), None), P(("groups", "cent"), None), P(("groups", "cent")))
    out_specs = (P(("groups", "pts"), "cent"), P(("groups", "cent"), "pts"))
    return jax.shard_map(
        per_device, mesh=mesh, in_specs=in_specs, out_specs=out_specs, check_vma=False
    )
```

```python
import functools

import jax
import jax.numpy as jnp
from jax import lax
from jax.experimental import pallas as pl
from jax.experimental.pallas import tpu as pltpu
from jax.sharding import PartitionSpec as P

MESH = pl.DeviceIdType.MESH
PIECES = 2
GROUP = 1
AHEAD = 2
LAG = 1
TILE = 512


def kernel(n, total_pts, x_ref, z_ref, alpha_ref, grads_ref, agop_ref,
           part, from_left, from_right, gall, acc, cnorm, wlow, t_core, t_own, t_x, t_send, t_mirror,
           send_r, send_l, recv_r, recv_l, gsend_r, gsend_l, grecv, tsend, trecv, *, pieces):
    me = lax.axis_index("cent")
    p = lax.axis_index("pts")
    chip, core = p // 2, lax.rem(p, 2)
    rows, width = x_ref.shape
    centres = z_ref.shape[0]
    rb = rows // pieces
    cols = width // n
    right = {"cent": jnp.minimum(me + 1, n - 1)}
    left = {"cent": jnp.maximum(me - 1, 0)}
    other_core = {"pts": chip * 2 + 1 - core}
    mirror = {"cent": p, "pts": me}
    other_chip = {"pts": (1 - chip) * 2 + core}
    has_left, has_right = me > 0, me < n - 1

    def here_made(s):
        return (me == s) | (has_left & ((s == 0) | (s > me)))

    def copy(src, dst, send, recv, target):
        return pltpu.make_async_remote_copy(
            src_ref=src, dst_ref=dst, send_sem=send, recv_sem=recv,
            device_id=target, device_id_type=MESH)

    def sum_r(r, d):
        return copy(part.at[r, d], from_left.at[r, d], send_r.at[r, d], recv_r.at[r, d], right)

    def sum_l(r, d):
        return copy(part.at[r, d], from_right.at[r, d], send_l.at[r, d], recv_l.at[r, d], left)

    def gather_r(r, s):
        return copy(gall.at[r, s], gall.at[r, s], gsend_r.at[r, s], grecv.at[r, s], right)

    def gather_l(r, s):
        return copy(gall.at[r, s], gall.at[r, s], gsend_l.at[r, s], grecv.at[r, s], left)

    barrier = pltpu.get_barrier_semaphore()

    @pl.when(has_left)
    def _():
        pl.semaphore_signal(barrier, inc=1, device_id=left, device_id_type=MESH)

    @pl.when(has_right)
    def _():
        pl.semaphore_signal(barrier, inc=1, device_id=right, device_id_type=MESH)

    pl.semaphore_signal(barrier, inc=1, device_id=other_core, device_id_type=MESH)
    pl.semaphore_signal(barrier, inc=1, device_id=other_chip, device_id_type=MESH)

    @pl.when(me != p)
    def _():
        pl.semaphore_signal(barrier, inc=1, device_id=mirror, device_id_type=MESH)

    @pl.loop(0, centres // 128)
    def _(i):
        at = pl.ds(pl.multiple_of(i * 128, 128), 128)
        zf = z_ref[at, :].astype(jnp.float32)
        sq = zf * zf
        lanes = sq[:, 0:128]
        for k in range(1, width // 128):
            lanes = lanes + sq[:, k * 128:(k + 1) * 128]
        cnorm[0:1, at] = jnp.sum(lanes.T, axis=0, keepdims=True)

    acc[...] = jnp.zeros_like(acc)

    def begin(r, d):
        @pl.when((me == 0) & (d > 0))
        def _():
            sum_r(r, d).start()

        @pl.when((me == n - 1) & (d < n - 1))
        def _():
            sum_l(r, d).start()

    def compute(g, waited):
        gr = GROUP * rb
        here = pl.ds(g * gr, gr)
        xf = x_ref[here, :].astype(jnp.float32)
        pnorm = jnp.sum(xf * xf, axis=1, keepdims=True)

        def tile(i, wsum):
            at = pl.ds(pl.multiple_of(i * TILE, TILE), TILE)
            cross = lax.dot_general(
                x_ref[here, :], z_ref[at, :], (((1,), (1,)), ((), ())),
                preferred_element_type=jnp.float32)
            dist = pnorm + cnorm[0:1, at] - 2.0 * cross
            weight = alpha_ref[0:1, at] * jnp.exp(dist * (-2.0 / width))
            wlow[:, at] = weight.astype(jnp.bfloat16)
            return wsum + jnp.sum(weight, axis=1, keepdims=True)

        wsum = lax.fori_loop(0, centres // TILE, tile, jnp.zeros((gr, 1), jnp.float32))
        if not waited:
            pl.semaphore_wait(barrier, 2 + has_left.astype(jnp.int32) + has_right.astype(jnp.int32)
                              + (me != p).astype(jnp.int32))

        @pl.loop(0, n)
        def _(k):
            d = jnp.where(me * 2 < n, n - 1 - k, k)
            at = pl.ds(pl.multiple_of(d * cols, cols), cols)
            term = jnp.dot(wlow[...], z_ref[:, at], preferred_element_type=jnp.float32)
            term = term - wsum * x_ref[here, at].astype(jnp.float32)
            for j in range(GROUP):
                r = g * GROUP + j
                part[r, d] = term[j * rb:(j + 1) * rb]

                if r < AHEAD:
                    begin(r, d)

    def scatter(r):
        for k in range(n):
            d = n - 1 - k

            @pl.when(has_left & (me < d))
            def _():
                sum_r(r, d).wait_recv()
                part[r, d] = part[r, d] + from_left[r, d]
                sum_r(r, d).start()

            @pl.when(has_right & (me > k))
            def _():
                sum_l(r, k).wait_recv()
                part[r, k] = part[r, k] + from_right[r, k]
                sum_l(r, k).start()

        @pl.when(has_left)
        def _():
            sum_r(r, me).wait_recv()
            part[r, me] = part[r, me] + from_left[r, me]

        @pl.when(has_right)
        def _():
            sum_l(r, me).wait_recv()
            part[r, me] = part[r, me] + from_right[r, me]

        mine = part[r, me] * (4.0 / width)
        gall[r, me] = mine
        grads_ref[r * rb:(r + 1) * rb, :] = mine

        @pl.when(me == 0)
        def _():
            gather_r(r, me).start()

        @pl.when(me > 1)
        def _():
            gather_l(r, me).start()

    def gather(r):
        @pl.when(has_left)
        def _():
            gather_r(r, 0).wait_recv()

            @pl.when(has_right)
            def _():
                gather_r(r, 0).start()

        for k in range(2, n):
            @pl.when(has_left & (me < k))
            def _():
                gather_l(r, k).wait_recv()

                @pl.when(me > 1)
                def _():
                    gather_l(r, k).start()

        def halves(value):
            high = value.astype(jnp.bfloat16)
            return high, (value - high.astype(jnp.float32)).astype(jnp.bfloat16)

        def times(a, b):
            return lax.dot_general(
                a, b, (((0,), (0,)), ((), ())), preferred_element_type=jnp.float32)

        high, low = halves(gall[r, me])

        @pl.loop(0, n)
        def _(s):
            @pl.when(here_made(s))
            def _():
                top, rest = halves(gall[r, s])
                acc[s] = acc[s] + (times(high, top) + (times(high, rest) + times(low, top)))

    compute(0, False)
    for r in range(pieces + LAG):
        if r == 0:
            compute(1, True)
        if r < pieces:
            scatter(r)
            if r + AHEAD < pieces:
                for k in range(n):
                    begin(r + AHEAD, jnp.where(me == 0, n - 1 - k, k))
        if r >= LAG:
            gather(r - LAG)

    far, near = (1 - chip) * 2, chip * 2
    one = copy(acc.at[far + 1 - core], t_core, tsend.at[0], trecv.at[0], other_core)
    two = copy(acc.at[near + 1 - core], t_own, tsend.at[1], trecv.at[1], other_core)
    three = copy(acc.at[far + core], t_x, tsend.at[2], trecv.at[2], other_chip)
    four = copy(t_send, t_mirror, tsend.at[3], trecv.at[3], mirror)

    @pl.when(here_made(far + 1 - core))
    def _():
        one.start()

    @pl.when(here_made(near + 1 - core))
    def _():
        two.start()

    @pl.when(here_made(far + core))
    def _():
        one.wait_recv()
        acc[far + core] = acc[far + core] + t_core[...]
        three.start()

    @pl.when(here_made(p))
    def _():
        two.wait_recv()
        own = acc[p] + t_own[...]
        three.wait_recv()
        own = (own + t_x[...]) / total_pts
        agop_ref[...] = own

        @pl.when(me != p)
        def _():
            t_send[...] = own.T
            four.start()
            four.wait_send()

    @pl.when(jnp.logical_not(here_made(p)))
    def _():
        four.wait_recv()
        agop_ref[...] = t_mirror[...]

    @pl.when(here_made(far + 1 - core))
    def _():
        one.wait_send()

    @pl.when(here_made(near + 1 - core))
    def _():
        two.wait_send()

    @pl.when(here_made(far + core))
    def _():
        three.wait_send()

    for r in range(pieces):
        for d in range(n):
            @pl.when(has_right & (me < d))
            def _():
                sum_r(r, d).wait_send()

            @pl.when(has_left & (me > d))
            def _():
                sum_l(r, d).wait_send()

            if d == 0:
                @pl.when(has_right)
                def _():
                    gather_r(r, d).wait_send()

            @pl.when((me > 1) & (me <= d))
            def _():
                gather_l(r, d).wait_send()


def fused(n, total_pts, points, centres, alpha):
    rows, width = points.shape
    cols, cen = width // n, centres.shape[0]
    rb = rows // PIECES
    chunks = pltpu.VMEM((PIECES, n, rb, cols), jnp.float32)
    block = pltpu.VMEM((cols, cols), jnp.float32)
    sems = pltpu.SemaphoreType.DMA((PIECES, n))
    vmem = pl.BlockSpec(memory_space=pltpu.VMEM)
    return pl.pallas_call(
        functools.partial(kernel, n, float(total_pts), pieces=PIECES),
        out_shape=(
            jax.ShapeDtypeStruct((rows, cols), jnp.float32),
            jax.ShapeDtypeStruct((cols, cols), jnp.float32),
        ),
        in_specs=[vmem] * 3,
        out_specs=(vmem, vmem),
        scratch_shapes=[
            chunks, chunks, chunks, chunks,
            pltpu.VMEM((n, cols, cols), jnp.float32),
            pltpu.VMEM((8, cen), jnp.float32),
            pltpu.VMEM((GROUP * rb, cen), jnp.bfloat16),
            block, block, block, block, block,
            sems, sems, sems, sems, sems, sems, sems,
            pltpu.SemaphoreType.DMA((4,)),
            pltpu.SemaphoreType.DMA((4,)),
        ],
        compiler_params=pltpu.CompilerParams(
            collective_id=0, has_side_effects=True, vmem_limit_bytes=48 * 1024 * 1024),
        cost_estimate=pl.CostEstimate(
            flops=4 * rows * width * cen, bytes_accessed=8 * 1024 * 1024,
            transcendentals=rows * cen),
    )(points, centres, alpha.reshape(1, cen))


def plain(total_pts, points, centres, alpha):
    width = points.shape[1]
    xf = points.astype(jnp.float32)
    zf = centres.astype(jnp.float32)
    pnorm = jnp.sum(xf * xf, axis=1)
    cross = jnp.dot(points, centres.T, preferred_element_type=jnp.float32)
    dist = pnorm[:, None] + jnp.sum(zf * zf, axis=1)[None, :] - 2.0 * cross
    weight = alpha[None, :] * jnp.exp(-2.0 * dist / width)
    wlow = weight.astype(jnp.bfloat16)
    partial_grad = (
        jnp.dot(wlow, centres, preferred_element_type=jnp.float32)
        - jnp.sum(weight, axis=1)[:, None] * xf
    )
    mine = lax.psum_scatter(partial_grad, "cent", scatter_dimension=1, tiled=True) * (4.0 / width)
    outer_rows = jnp.dot(
        mine.T,
        lax.all_gather(mine, "cent", axis=1, tiled=True),
        precision=lax.Precision.HIGHEST,
        preferred_element_type=jnp.float32,
    )
    agop = lax.psum_scatter(outer_rows, "pts", scatter_dimension=1, tiled=True) / total_pts
    return (mine, agop)


def solution(mesh):
    n, npts = mesh.shape["cent"], mesh.shape["pts"]

    def per_device(points, centres, alpha):
        rows, width = points.shape
        total_pts = rows * npts
        fits = (n == npts == 4 and width % (128 * n) == 0
                and rows % (16 * PIECES) == 0 and centres.shape[0] % TILE == 0)
        if fits:
            return fused(n, total_pts, points, centres, alpha)
        return plain(total_pts, points, centres, alpha)

    in_specs = (P(("groups", "pts"), None), P(("groups", "cent"), None), P(("groups", "cent")))
    out_specs = (P(("groups", "pts"), "cent"), P(("groups", "cent"), "pts"))
    return jax.shard_map(
        per_device, mesh=mesh, in_specs=in_specs, out_specs=out_specs, check_vma=False
    )
```
